32 devices in a mesh: ctx: 8 (over y, x, core), tp: 4 (over z).
Axes of the slice: x: 2, y: 2, z: 4, core: 2. Of those that a mesh axis runs over, the one named last changes fastest.
Arguments:
- features: bfloat16 [3, 2048, 8192], P(None, 'ctx', 'tp'), may hold values from -6 to 6
- short_taps: bfloat16 [3, 512, 7], P(None, 'tp'), may hold values from -2 to 2
- long_taps: bfloat16 [512, 128], P('tp'), may hold values from -0.5 to 0.5
- skip_gain: bfloat16 [8192], P('tp'), may hold values from -4 to 4
- cotangent: bfloat16 [2048, 8192], P('ctx', 'tp'), may hold values from -6 to 6
Outputs:
- gated: bfloat16 [2048, 8192], P('ctx', 'tp')
- feature_grad: bfloat16 [3, 2048, 8192], P(None, 'ctx', 'tp')
- short_grad: float32 [3, 512, 7], P(None, 'tp')
- long_grad: float32 [512, 128], P('tp')
- skip_grad: float32 [8192], P('tp')
The draws below stay inside these ranges and needn't reach their ends.
All inputs are finite; a program needn't handle non-finite values.
Results may differ from the reference program's by a relative error of at most 0.0074.
Values may be sent and summed in bfloat16 or wider, within the bound.
A program may use at most 128 MiB of HBM per device.

```python
import math
import jax
import jax.numpy as jnp
from jax import lax

D = 8192
SHORT = 7
LONG = 128
G = 512
TOKENS = 2048


def steps_of(own_key, extent, split, least, largest):
    level = 1.0
    for dim, parts in split:
        heights = jax.random.uniform(jax.random.fold_in(jax.random.fold_in(own_key, 6), dim), (parts,), jnp.float32, least / len(split), largest / len(split))
        level = level * jnp.repeat(jnp.exp(heights), extent[dim] // parts).reshape((-1,) + (1,) * (len(extent) - 1 - dim))
    return level


def scatter_about(rng, shape, scale, reach, cuts=(), held_as=jnp.bfloat16):
    factor_of = steps_of(rng, shape, cuts, -0.22, 0.18) if cuts else 1.0
    entries = jax.random.normal(rng, shape, jnp.float32) * scale * factor_of
    return jnp.minimum(jnp.maximum(entries, -reach), reach).astype(held_as)


def setup_inputs(seed: int = 0) -> dict:
    keys = jax.random.split(jax.random.key(seed), 6)
    return {
        "features": scatter_about(keys[0], (3, TOKENS, D), 1.0, 6.0, ((1, 8), (2, 4))),
        "short_taps": scatter_about(keys[1], (3, G, SHORT), SHORT ** -0.5, 2.0, ((1, 4),)),
        "long_taps": scatter_about(keys[2], (G, LONG), LONG ** -0.5, 0.5, ((0, 4),)),
        "skip_gain": scatter_about(keys[3], (D,), 1.0, 4.0, ((0, 4),)),
        "cotangent": scatter_about(keys[4], (TOKENS, D), 1.0, 6.0, ((0, 8), (1, 4))),
    }


def settle(values):
    return lax.optimization_barrier(values)

def causal_short(padded, taps, rows):
    total = jnp.zeros((rows,) + padded.shape[1:], jnp.float32)
    for offset in range(7):
        total = total + taps[:, :, offset] * padded[6 - offset:6 - offset + rows].astype(jnp.float32)
    return total

def block_pass(zblock, short_block, long_block, gain_block, grad_block):
    rows = zblock.shape[0]
    width = zblock.shape[2]
    taps = jnp.repeat(short_block, 16, axis=1).astype(jnp.float32)
    padded = jnp.concatenate([jnp.zeros((6, 3, width), zblock.dtype), zblock], axis=0)
    mixed = settle(causal_short(padded, taps, rows).astype(jnp.bfloat16))
    query = mixed[:, 0].astype(jnp.float32)
    key = mixed[:, 1].astype(jnp.float32)
    value = mixed[:, 2].astype(jnp.float32)
    product = settle((key * value).astype(jnp.bfloat16))
    prod_f = product.astype(jnp.float32)
    length = rows + 128
    filt = jnp.repeat(long_block, 16, axis=0).astype(jnp.float32).T
    spectrum = jnp.fft.rfft(filt, n=length, axis=0)
    prod_spec = jnp.fft.rfft(prod_f, n=length, axis=0)
    conv = jnp.fft.irfft(prod_spec * spectrum, n=length, axis=0)[:rows]
    gain = gain_block.astype(jnp.float32)
    inner = conv + gain * prod_f
    gated = (query * inner).astype(jnp.bfloat16)
    grad_in = grad_block.astype(jnp.float32)
    grad_query = grad_in * inner
    grad_inner = settle((grad_in * query).astype(jnp.bfloat16))
    inner_f = grad_inner.astype(jnp.float32)
    inner_spec = jnp.fft.rfft(inner_f, n=length, axis=0)
    back = jnp.fft.irfft(inner_spec * jnp.conj(spectrum), n=length, axis=0)[:rows]
    grad_product = settle((back + gain * inner_f).astype(jnp.bfloat16))
    product_g = grad_product.astype(jnp.float32)
    grad_mixed = settle(jnp.stack([grad_query, product_g * value, product_g * key], axis=1).astype(jnp.bfloat16))
    mixed_g = grad_mixed.astype(jnp.float32)
    trailing = jnp.concatenate([mixed_g, jnp.zeros((6, 3, width), jnp.float32)], axis=0)
    feature_grad = jnp.zeros((rows, 3, width), jnp.float32)
    for offset in range(7):
        feature_grad = feature_grad + taps[:, :, offset] * trailing[offset:offset + rows]
    feature_grad = feature_grad.astype(jnp.bfloat16)
    corr = jnp.fft.irfft(inner_spec * jnp.conj(prod_spec), n=length, axis=0)[:128]
    long_grad = corr.T.reshape(width // 16, 16, 128).sum(axis=1)
    skip_grad = lax.optimization_barrier(jnp.sum(inner_f * prod_f, axis=0))
    short_all = jnp.stack([lax.optimization_barrier(jnp.sum(mixed_g * padded[6 - offset:6 - offset + rows].astype(jnp.float32), axis=0)) for offset in range(7)], axis=-1)
    short_grad = short_all.reshape(3, width // 16, 16, 7).sum(axis=2)
    return (gated, feature_grad, short_grad, long_grad, skip_grad)

def reference(features, short_taps, long_taps, skip_gain, cotangent):
    block = min(D, 512)
    count = D // block
    init = (jnp.zeros((TOKENS, D), jnp.bfloat16), jnp.zeros((3, TOKENS, D), jnp.bfloat16), jnp.zeros((3, G, 7), jnp.float32), jnp.zeros((G, 128), jnp.float32), jnp.zeros((D,), jnp.float32))

    def step(index, carry):
        start = (index * block).astype(jnp.int32)
        gstart = (index * (block // 16)).astype(jnp.int32)
        zblock = jnp.transpose(lax.dynamic_slice_in_dim(features, start, block, 2), (1, 0, 2))
        short_block = lax.dynamic_slice_in_dim(short_taps, gstart, block // 16, 1)
        long_block = lax.dynamic_slice_in_dim(long_taps, gstart, block // 16, 0)
        gain_block = lax.dynamic_slice_in_dim(skip_gain, start, block, 0)
        grad_block = lax.dynamic_slice_in_dim(cotangent, start, block, 1)
        gated, feature_grad, short_grad, long_grad, skip_grad = block_pass(zblock, short_block, long_block, gain_block, grad_block)
        return (lax.dynamic_update_slice_in_dim(carry[0], gated, start, 1), lax.dynamic_update_slice_in_dim(carry[1], jnp.transpose(feature_grad, (1, 0, 2)), start, 2), lax.dynamic_update_slice_in_dim(carry[2], short_grad, gstart, 1), lax.dynamic_update_slice_in_dim(carry[3], long_grad, gstart, 0), lax.dynamic_update_slice_in_dim(carry[4], skip_grad, start, 0))
    gated, feature_grad, short_grad, long_grad, skip_grad = lax.fori_loop(0, count, step, init)
    group_scale = 1.0 / math.sqrt(16.0 * TOKENS)
    token_scale = 1.0 / math.sqrt(1.0 * TOKENS)
    return (gated, feature_grad, short_grad * group_scale, long_grad * group_scale, skip_grad * token_scale)
```

```python
import functools
import math

import jax
import jax.numpy as jnp
from jax import lax
from jax.experimental import pallas as pl
from jax.experimental.pallas import tpu as pltpu
from jax.sharding import PartitionSpec as P

F32 = jnp.float32
BF16 = jnp.bfloat16
LANES = 128
EDGE = 16
CHUNK = 64
MESH = pl.DeviceIdType.MESH
EXACT = lax.Precision.HIGHEST


def lanes_of(tile):
    return pl.ds(pl.multiple_of(tile * LANES, LANES), LANES)


def spread(row, width):
    wide = jnp.concatenate([row, jnp.zeros_like(row)], axis=1)
    return jnp.broadcast_to(wide, (LANES, width))


def kernel(
    n,
    tiles,
    rows,
    reduce_here,
    feat_ref,
    taps_ref,
    long_ref,
    gain_ref,
    cot_ref,
    gated_ref,
    fgrad_ref,
    red_out,
    edge,
    padf,
    mixed,
    prod,
    gi,
    gm,
    gmf,
    causal,
    ahead,
    flipped,
    red_in,
    red_recv,
    edge_sem,
    tail_sem,
    head_sem,
    gm_sem,
    scatter_sem,
    gather_sem,
):
    me = lax.axis_index("ctx")
    nxt = lax.rem(me + 1, n)
    prv = lax.rem(me + n - 1, n)
    has_prev = me > 0
    has_next = me < n - 1
    groups = 8 * tiles
    units = red_out.shape[0]
    share = units // n if reduce_here else 0

    def remote(src, dst, sems, index, device):
        return pltpu.make_async_remote_copy(
            src_ref=src,
            dst_ref=dst,
            send_sem=sems.at[0, index],
            recv_sem=sems.at[1, index],
            device_id={"ctx": device},
            device_id_type=MESH,
        )

    def edge_copy():
        return remote(feat_ref.at[:, pl.ds(rows - EDGE, EDGE)], edge, edge_sem, 0, nxt)

    def tail_copy(t):
        return remote(
            prod.at[t, pl.ds(rows, LANES)], prod.at[t, pl.ds(0, LANES)], tail_sem, t, nxt
        )

    def head_copy(t):
        return remote(gi.at[t, pl.ds(0, LANES)], gi.at[t, pl.ds(rows, LANES)], head_sem, t, prv)

    def gm_copy(t):
        return remote(
            gm.at[t, :, pl.ds(0, EDGE)], gm.at[t, :, pl.ds(rows, EDGE)], gm_sem, t, prv
        )

    def scatter_copy(k):
        peer = lax.rem(me + k, n)
        return remote(
            red_in.at[pl.ds(peer * share, share)], red_recv.at[k - 1], scatter_sem, k - 1, peer
        )

    def gather_copy(k):
        peer = lax.rem(me + k, n)
        mine = red_out.at[pl.ds(me * share, share)]
        return remote(mine, mine, gather_sem, k - 1, peer)

    barrier = pltpu.get_barrier_semaphore()
    if reduce_here:
        for k in range(1, n):
            pl.semaphore_signal(
                barrier, inc=1, device_id={"ctx": lax.rem(me + k, n)}, device_id_type=MESH
            )
        pl.semaphore_wait(barrier, n - 1)
    else:

        @pl.when(has_prev)
        def _():
            pl.semaphore_signal(barrier, inc=1, device_id={"ctx": prv}, device_id_type=MESH)

        @pl.when(has_next)
        def _():
            pl.semaphore_signal(barrier, inc=1, device_id={"ctx": nxt}, device_id_type=MESH)

        @pl.when(has_prev)
        def _():
            pl.semaphore_wait(barrier, 1)

        @pl.when(has_next)
        def _():
            pl.semaphore_wait(barrier, 1)

    @pl.when(has_next)
    def _():
        edge_copy().start()

    @pl.when(jnp.logical_not(has_prev))
    def _():
        edge[...] = jnp.zeros_like(edge)
        prod[:, :LANES] = jnp.zeros((tiles, LANES, LANES), BF16)

    @pl.when(jnp.logical_not(has_next))
    def _():
        gi[:, rows:] = jnp.zeros((tiles, LANES, LANES), BF16)
        gm[:, :, rows:] = jnp.zeros((tiles, 3, EDGE, LANES), BF16)

    anti = (
        lax.broadcasted_iota(jnp.int32, (LANES, LANES), 0)
        + lax.broadcasted_iota(jnp.int32, (LANES, LANES), 1)
        == LANES - 1
    ).astype(F32)
    anti_b = anti.astype(BF16)
    flipped[...] = jnp.dot(long_ref[...], anti_b, preferred_element_type=F32)

    def build_causal(t, carry):
        part = flipped[pl.ds(pl.multiple_of(t * 8, 8), 8), :]
        for g in range(8):
            causal[t, g] = pltpu.roll(
                spread(part[g : g + 1], 2 * LANES), 1, 1, stride=1, stride_axis=0
            ).astype(BF16)
        return carry

    lax.fori_loop(0, tiles, build_causal, 0)

    @pl.when(has_prev)
    def _():
        edge_copy().wait_recv()

    def front(t, carry):
        cols = lanes_of(t)
        for i in range(3):
            padf[t, i, :EDGE] = edge[i, :, cols].astype(F32)
            padf[t, i, EDGE:] = feat_ref[i, :, cols].astype(F32)
        for start in range(0, rows, CHUNK):
            values = []
            for i in range(3):
                total = jnp.zeros((CHUNK, LANES), F32)
                for j in range(7):
                    total = total + taps_ref[i, pl.ds(j, 1), cols] * padf[
                        t, i, pl.ds(EDGE - j + start, CHUNK)
                    ]
                rounded = total.astype(BF16)
                mixed[t, i, pl.ds(start, CHUNK)] = rounded
                values.append(rounded.astype(F32))
            query, key, value = values
            prod[t, pl.ds(LANES + start, CHUNK)] = (key * value).astype(BF16)
            grad_in = cot_ref[pl.ds(start, CHUNK), cols].astype(F32)
            gi[t, pl.ds(start, CHUNK)] = (grad_in * query).astype(BF16)

        @pl.when(has_next)
        def _():
            tail_copy(t).start()

        @pl.when(has_prev)
        def _():
            head_copy(t).start()

        return carry

    lax.fori_loop(0, tiles, front, 0)

    flipped[...] = long_ref[...].astype(F32)

    def build_ahead(t, carry):
        part = flipped[pl.ds(pl.multiple_of(t * 8, 8), 8), :]
        for g in range(8):
            ahead[t, g] = pltpu.roll(
                spread(part[g : g + 1], 2 * LANES), 0, 1, stride=1, stride_axis=0
            ).astype(BF16)
        return carry

    lax.fori_loop(0, tiles, build_ahead, 0)

    lane_group = lax.rem(
        lax.broadcasted_iota(jnp.int32, (LANES, 2 * LANES), 1), LANES
    ) // 16
    blocks = rows // LANES

    def pair(ref, t, first):
        return jnp.concatenate(
            [ref[t, pl.ds(first, LANES)], ref[t, pl.ds(first + LANES, LANES)]], axis=1
        )

    def middle(t, short_acc):
        cols = lanes_of(t)

        @pl.when(has_prev)
        def _():
            tail_copy(t).wait_recv()

        @pl.when(has_next)
        def _():
            head_copy(t).wait_recv()

        gain = gain_ref[:, cols].astype(F32)
        skip = jnp.zeros((8, LANES), F32)
        folds = [jnp.zeros((1, LANES), F32)] * 8
        for first in range(0, rows, 2 * LANES):
            span = 2 * LANES
            window = jnp.concatenate(
                [prod[t, pl.ds(first, span)], prod[t, pl.ds(first + LANES, span)]], axis=1
            )
            coming = jnp.concatenate(
                [gi[t, pl.ds(first, span)], gi[t, pl.ds(first + LANES, span)]], axis=1
            )
            conv = jnp.zeros((LANES, 2 * LANES), F32)
            back = jnp.zeros((LANES, 2 * LANES), F32)
            turned = jnp.dot(anti_b, pair(gi, t, first), preferred_element_type=F32)
            for g in range(8):
                own = lane_group == g
                one = jnp.dot(causal[t, g], window, preferred_element_type=F32)
                conv = jnp.where(own, one, conv)
                two = jnp.dot(ahead[t, g], coming, preferred_element_type=F32)
                back = jnp.where(own, two, back)
                grid = lax.dot_general(
                    jnp.where(own, turned, 0.0).astype(BF16),
                    window,
                    (((1,), (1,)), ((), ())),
                    preferred_element_type=F32,
                )
                lined = pltpu.roll(grid, 0, 1, stride=1, stride_axis=0)
                folds[g] = folds[g] + jnp.sum(lined[:, LANES:], axis=0, keepdims=True)
            for half in range(2):
                start = first + half * LANES
                here = slice(half * LANES, (half + 1) * LANES)
                at = pl.ds(start, LANES)
                product = prod[t, pl.ds(start + LANES, LANES)].astype(F32)
                grad_inner = gi[t, at].astype(F32)
                query = mixed[t, 0, at].astype(F32)
                key = mixed[t, 1, at].astype(F32)
                value = mixed[t, 2, at].astype(F32)
                inner = conv[:, here] + gain * product
                gated_ref[at, cols] = (query * inner).astype(BF16)
                gm[t, 0, at] = (cot_ref[at, cols].astype(F32) * inner).astype(BF16)
                grad_prod = (back[:, here] + gain * grad_inner).astype(BF16).astype(F32)
                gm[t, 1, at] = (grad_prod * value).astype(BF16)
                gm[t, 2, at] = (grad_prod * key).astype(BF16)
                skip = skip + jnp.sum(
                    (grad_inner * product).reshape(LANES // 8, 8, LANES), axis=0
                )

        @pl.when(has_prev)
        def _():
            gm_copy(t).start()

        red_in[t] = jnp.concatenate(folds, axis=0)
        red_in[tiles + t // 8, pl.ds(lax.rem(t, 8), 1)] = jnp.sum(skip, axis=0, keepdims=True)
        sums = []
        for i in range(3):
            parts = [jnp.zeros((8, LANES), F32)] * 7
            for start in range(0, rows, CHUNK):
                grad = gm[t, i, pl.ds(start, CHUNK)].astype(F32)
                for j in range(7):
                    term = grad * padf[t, i, pl.ds(EDGE - j + start, CHUNK)]
                    parts[j] = parts[j] + jnp.sum(term.reshape(CHUNK // 8, 8, LANES), axis=0)
            sums += [jnp.sum(part, axis=0, keepdims=True) for part in parts]
            sums.append(jnp.zeros((1, LANES), F32))
        member = (
            lax.broadcasted_iota(jnp.int32, (LANES, LANES), 0) // 16 + t * 8
            == lax.broadcasted_iota(jnp.int32, (LANES, LANES), 1)
        ).astype(F32)
        return short_acc + jnp.dot(
            jnp.concatenate(sums, axis=0), member, precision=EXACT, preferred_element_type=F32
        )

    skip_units = (tiles + 7) // 8
    red_in[tiles:] = jnp.zeros((units - tiles, 8, LANES), F32)
    short_sum = lax.fori_loop(0, tiles, middle, jnp.zeros((24, LANES), F32))
    at_short = tiles + skip_units
    red_in[at_short : at_short + 3] = short_sum.reshape(3, 8, LANES)
    lags = red_in[:tiles].reshape(groups, LANES)
    lags = jnp.dot(lags, anti, precision=EXACT, preferred_element_type=F32)
    red_in[:tiles] = lags.reshape(tiles, 8, LANES)
    if reduce_here:
        for k in range(1, n):
            scatter_copy(k).start()
    else:
        red_out[...] = red_in[...]

    def finish(t, carry):
        cols = lanes_of(t)

        @pl.when(has_next)
        def _():
            gm_copy(t).wait_recv()

        for i in range(3):
            gmf[i] = gm[t, i].astype(F32)
        for start in range(0, rows, CHUNK):
            for i in range(3):
                total = jnp.zeros((CHUNK, LANES), F32)
                for j in range(7):
                    total = total + taps_ref[i, pl.ds(j, 1), cols] * gmf[
                        i, pl.ds(start + j, CHUNK)
                    ]
                fgrad_ref[i, pl.ds(start, CHUNK), cols] = total.astype(BF16)
        return carry

    if reduce_here:
        half = tiles // 2
        lax.fori_loop(0, half, finish, 0)
        total = red_in[pl.ds(me * share, share)]
        for k in range(1, n):
            scatter_copy(k).wait_recv()
            total = total + red_recv[k - 1]
        red_out[pl.ds(me * share, share)] = total
        for k in range(1, n):
            gather_copy(k).start()
        lax.fori_loop(half, tiles, finish, 0)
    else:
        lax.fori_loop(0, tiles, finish, 0)

    @pl.when(has_next)
    def _():
        edge_copy().wait_send()

    def drain(t, carry):
        @pl.when(has_next)
        def _():
            tail_copy(t).wait_send()

        @pl.when(has_prev)
        def _():
            head_copy(t).wait_send()
            gm_copy(t).wait_send()

        return carry

    lax.fori_loop(0, tiles, drain, 0)
    if reduce_here:
        for k in range(1, n):
            scatter_copy(k).wait_send()
            gather_copy(k).wait()


def body(features, short_taps, long_taps, skip_gain, cotangent):
    rows, width = features.shape[1:]
    tiles = width // LANES
    groups = width // 16
    n = lax.axis_size("ctx")
    skip_units = (tiles + 7) // 8
    units = tiles + skip_units + 3
    reduce_here = n <= 16
    if reduce_here:
        units = -(-units // n) * n
    share = units // n if reduce_here else 1
    peers = n - 1 if reduce_here else 1
    taps = jnp.repeat(jnp.transpose(short_taps, (0, 2, 1)).astype(F32), 16, axis=2)
    vmem = pl.BlockSpec(memory_space=pltpu.VMEM)
    gated, fgrad, red = pl.pallas_call(
        functools.partial(kernel, n, tiles, rows, reduce_here),
        out_shape=(
            jax.ShapeDtypeStruct((rows, width), BF16),
            jax.ShapeDtypeStruct((3, rows, width), BF16),
            jax.ShapeDtypeStruct((units, 8, LANES), F32),
        ),
        in_specs=[vmem] * 5,
        out_specs=(vmem, vmem, vmem),
        scratch_shapes=[
            pltpu.VMEM((3, EDGE, width), BF16),
            pltpu.VMEM((tiles, 3, EDGE + rows, LANES), F32),
            pltpu.VMEM((tiles, 3, rows, LANES), BF16),
            pltpu.VMEM((tiles, LANES + rows, LANES), BF16),
            pltpu.VMEM((tiles, rows + LANES, LANES), BF16),
            pltpu.VMEM((tiles, 3, rows + EDGE, LANES), BF16),
            pltpu.VMEM((3, rows + EDGE, LANES), F32),
            pltpu.VMEM((tiles, 8, LANES, 2 * LANES), BF16),
            pltpu.VMEM((tiles, 8, LANES, 2 * LANES), BF16),
            pltpu.VMEM((groups, LANES), F32),
            pltpu.VMEM((units, 8, LANES), F32),
            pltpu.VMEM((peers, share, 8, LANES), F32),
            pltpu.SemaphoreType.DMA((2, 1)),
            pltpu.SemaphoreType.DMA((2, tiles)),
            pltpu.SemaphoreType.DMA((2, tiles)),
            pltpu.SemaphoreType.DMA((2, tiles)),
            pltpu.SemaphoreType.DMA((2, peers)),
            pltpu.SemaphoreType.DMA((2, peers)),
        ],
        compiler_params=pltpu.CompilerParams(
            collective_id=0, has_side_effects=True, vmem_limit_bytes=60 * 1024 * 1024
        ),
        cost_estimate=pl.CostEstimate(
            flops=12 * rows * width * LANES * 8, bytes_accessed=16 * rows * width, transcendentals=0
        ),
    )(features, taps, long_taps, skip_gain.reshape(1, width), cotangent)
    if not reduce_here:
        red = lax.psum(red, "ctx")
    total = rows * n
    group_scale = 1.0 / math.sqrt(16.0 * total)
    token_scale = 1.0 / math.sqrt(1.0 * total)
    long_grad = red[:tiles].reshape(groups, LANES) * group_scale
    skip_grad = red[tiles : tiles + skip_units].reshape(-1)[:width] * token_scale
    short = red[tiles + skip_units : tiles + skip_units + 3]
    short_grad = jnp.transpose(short[:, :7, :groups], (0, 2, 1)) * group_scale
    return gated, fgrad, short_grad, long_grad, skip_grad


def solution(mesh):
    placed = (P(None, "ctx", "tp"), P(None, "tp", None), P("tp", None), P("tp"), P("ctx", "tp"))
    return jax.shard_map(
        body,
        mesh=mesh,
        in_specs=placed,
        out_specs=(
            P("ctx", "tp"),
            P(None, "ctx", "tp"),
            P(None, "tp", None),
            P("tp", None),
            P("tp"),
        ),
        check_vma=False,
    )
```

```python
import functools
import math

import jax
import jax.numpy as jnp
from jax import lax
from jax.experimental import pallas as pl
from jax.experimental.pallas import tpu as pltpu
from jax.sharding import PartitionSpec as P

F32 = jnp.float32
BF16 = jnp.bfloat16
LANES = 128
EDGE = 16
CHUNK = 64
MESH = pl.DeviceIdType.MESH
EXACT = lax.Precision.HIGHEST


def lanes_of(tile):
    return pl.ds(pl.multiple_of(tile * LANES, LANES), LANES)


def tile_taps(taps_ref, tile):
    groups = taps_ref.shape[2]
    member = (
        lax.broadcasted_iota(jnp.int32, (groups, LANES), 0)
        == lax.broadcasted_iota(jnp.int32, (groups, LANES), 1) // 16 + tile * 8
    ).astype(F32).astype(BF16)
    return [jnp.dot(taps_ref[i], member, preferred_element_type=F32) for i in range(3)]


def circulant(row, shift):
    return pltpu.roll(
        jnp.broadcast_to(row, (LANES, LANES)), shift, 1, stride=1, stride_axis=0
    )


def kernel(
    n,
    tiles,
    rows,
    reduce_here,
    feat_ref,
    taps_ref,
    long_ref,
    gain_ref,
    cot_ref,
    gated_ref,
    gm,
    red_out,
    edge,
    padf,
    mixed,
    prod,
    gi,
    causal,
    ahead,
    flipped,
    gainf,
    red_in,
    red_recv,
    edge_sem,
    tail_sem,
    head_sem,
    gm_sem,
    scatter_sem,
    gather_sem,
):
    me = lax.axis_index("ctx")
    nxt = lax.rem(me + 1, n)
    prv = lax.rem(me + n - 1, n)
    has_prev = me > 0
    has_next = me < n - 1
    groups = 8 * tiles
    units = red_out.shape[0]
    share = units // n if reduce_here else 0

    def remote(src, dst, sems, index, device):
        return pltpu.make_async_remote_copy(
            src_ref=src,
            dst_ref=dst,
            send_sem=sems.at[0, index],
            recv_sem=sems.at[1, index],
            device_id={"ctx": device},
            device_id_type=MESH,
        )

    def edge_copy():
        return remote(feat_ref.at[:, pl.ds(rows - EDGE, EDGE)], edge, edge_sem, 0, nxt)

    def tail_copy(t):
        return remote(
            prod.at[t, pl.ds(rows, LANES)], prod.at[t, pl.ds(0, LANES)], tail_sem, t, nxt
        )

    def head_copy(t):
        return remote(gi.at[t, pl.ds(0, LANES)], gi.at[t, pl.ds(rows, LANES)], head_sem, t, prv)

    def gm_copy(t):
        return remote(
            gm.at[t, :, pl.ds(0, EDGE)], gm.at[t, :, pl.ds(rows, EDGE)], gm_sem, t, prv
        )

    def scatter_copy(k):
        peer = lax.rem(me + k, n)
        return remote(
            red_in.at[pl.ds(peer * share, share)], red_recv.at[k - 1], scatter_sem, k - 1, peer
        )

    def gather_copy(k):
        peer = lax.rem(me + k, n)
        mine = red_out.at[pl.ds(me * share, share)]
        return remote(mine, mine, gather_sem, k - 1, peer)

    barrier = pltpu.get_barrier_semaphore()
    if reduce_here:
        for k in range(1, n):
            pl.semaphore_signal(
                barrier, inc=1, device_id={"ctx": lax.rem(me + k, n)}, device_id_type=MESH
            )
        pl.semaphore_wait(barrier, n - 1)
    else:

        @pl.when(has_prev)
        def _():
            pl.semaphore_signal(barrier, inc=1, device_id={"ctx": prv}, device_id_type=MESH)

        @pl.when(has_next)
        def _():
            pl.semaphore_signal(barrier, inc=1, device_id={"ctx": nxt}, device_id_type=MESH)

        @pl.when(has_prev)
        def _():
            pl.semaphore_wait(barrier, 1)

        @pl.when(has_next)
        def _():
            pl.semaphore_wait(barrier, 1)

    @pl.when(has_next)
    def _():
        edge_copy().start()

    @pl.when(jnp.logical_not(has_prev))
    def _():
        edge[...] = jnp.zeros_like(edge)
        prod[:, :LANES] = jnp.zeros((tiles, LANES, LANES), BF16)

    @pl.when(jnp.logical_not(has_next))
    def _():
        gi[:, rows:] = jnp.zeros((tiles, LANES, LANES), BF16)
        gm[:, :, rows:] = jnp.zeros((tiles, 3, EDGE, LANES), BF16)

    row_pos = lax.broadcasted_iota(jnp.int32, (LANES, LANES), 0)
    col_pos = lax.broadcasted_iota(jnp.int32, (LANES, LANES), 1)
    above = col_pos > row_pos
    below = col_pos < row_pos
    past = col_pos + row_pos > LANES - 1
    anti = (row_pos + col_pos == LANES - 1).astype(F32)
    anti_b = anti.astype(BF16)
    flipped[...] = jnp.dot(long_ref[...], anti_b, preferred_element_type=F32)

    def build_causal(t, carry):
        part = flipped[pl.ds(pl.multiple_of(t * 8, 8), 8), :]
        for g in range(8):
            turned = circulant(part[g : g + 1], 1)
            causal[t, g, :, :LANES] = jnp.where(above, turned, 0.0).astype(BF16)
            causal[t, g, :, LANES:] = jnp.where(above, 0.0, turned).astype(BF16)
        return carry

    lax.fori_loop(0, tiles, build_causal, 0)

    @pl.when(has_prev)
    def _():
        edge_copy().wait_recv()

    gainf[...] = gain_ref[...].astype(F32)

    def front(t, carry):
        cols = lanes_of(t)
        taps = tile_taps(taps_ref, t)
        for i in range(3):
            padf[t, i, :EDGE] = edge[i, :, cols].astype(F32)
            padf[t, i, EDGE:] = feat_ref[i, :, cols].astype(F32)
        for start in range(0, rows, CHUNK):
            values = []
            for i in range(3):
                total = jnp.zeros((CHUNK, LANES), F32)
                for j in range(7):
                    total = total + taps[i][j : j + 1] * padf[
                        t, i, pl.ds(EDGE - j + start, CHUNK)
                    ]
                rounded = total.astype(BF16)
                mixed[t, i, pl.ds(start, CHUNK)] = rounded
                values.append(rounded.astype(F32))
            query, key, value = values
            prod[t, pl.ds(LANES + start, CHUNK)] = (key * value).astype(BF16)
            grad_in = cot_ref[pl.ds(start, CHUNK), cols].astype(F32)
            gi[t, pl.ds(start, CHUNK)] = (grad_in * query).astype(BF16)

        @pl.when(has_next)
        def _():
            tail_copy(t).start()

        @pl.when(has_prev)
        def _():
            head_copy(t).start()

        return carry

    lax.fori_loop(0, tiles, front, 0)

    flipped[...] = long_ref[...].astype(F32)

    def build_ahead(t, carry):
        part = flipped[pl.ds(pl.multiple_of(t * 8, 8), 8), :]
        for g in range(8):
            turned = circulant(part[g : g + 1], 0)
            ahead[t, g, :, :LANES] = jnp.where(below, 0.0, turned).astype(BF16)
            ahead[t, g, :, LANES:] = jnp.where(below, turned, 0.0).astype(BF16)
        return carry

    lax.fori_loop(0, tiles, build_ahead, 0)

    lane_group = lax.rem(
        lax.broadcasted_iota(jnp.int32, (LANES, 2 * LANES), 1), LANES
    ) // 16
    blocks = rows // LANES

    def pair(ref, t, first):
        return jnp.concatenate(
            [ref[t, pl.ds(first, LANES)], ref[t, pl.ds(first + LANES, LANES)]], axis=1
        )

    def middle(t, short_acc):
        cols = lanes_of(t)

        @pl.when(has_prev)
        def _():
            tail_copy(t).wait_recv()

        @pl.when(has_next)
        def _():
            head_copy(t).wait_recv()

        gain = gainf[pl.ds(t, 1)]
        skip = jnp.zeros((8, LANES), F32)
        folds = [jnp.zeros((1, LANES), F32)] * 8
        for first in range(0, rows, 2 * LANES):
            span = 2 * LANES
            window = jnp.concatenate(
                [prod[t, pl.ds(first, span)], prod[t, pl.ds(first + LANES, span)]], axis=1
            )
            coming = jnp.concatenate(
                [gi[t, pl.ds(first, span)], gi[t, pl.ds(first + LANES, span)]], axis=1
            )
            conv = jnp.zeros((LANES, 2 * LANES), F32)
            back = jnp.zeros((LANES, 2 * LANES), F32)
            turned = jnp.dot(anti_b, pair(gi, t, first), preferred_element_type=F32)
            for g in range(8):
                own = lane_group == g
                one = jnp.dot(causal[t, g], window, preferred_element_type=F32)
                conv = jnp.where(own, one, conv)
                two = jnp.dot(ahead[t, g], coming, preferred_element_type=F32)
                back = jnp.where(own, two, back)
                grid = lax.dot_general(
                    jnp.where(own, turned, 0.0).astype(BF16),
                    window,
                    (((1,), (1,)), ((), ())),
                    preferred_element_type=F32,
                )
                ring = jnp.where(past, grid[:, :LANES], grid[:, LANES:])
                lined = pltpu.roll(ring, 0, 1, stride=1, stride_axis=0)
                folds[g] = folds[g] + jnp.sum(lined, axis=0, keepdims=True)
            for half in range(2):
                start = first + half * LANES
                here = slice(half * LANES, (half + 1) * LANES)
                at = pl.ds(start, LANES)
                product = prod[t, pl.ds(start + LANES, LANES)].astype(F32)
                grad_inner = gi[t, at].astype(F32)
                query = mixed[t, 0, at].astype(F32)
                key = mixed[t, 1, at].astype(F32)
                value = mixed[t, 2, at].astype(F32)
                inner = conv[:, here] + gain * product
                gated_ref[t, at] = (query * inner).astype(BF16)
                gm[t, 0, at] = (cot_ref[at, cols].astype(F32) * inner).astype(BF16)
                grad_prod = (back[:, here] + gain * grad_inner).astype(BF16).astype(F32)
                gm[t, 1, at] = (grad_prod * value).astype(BF16)
                gm[t, 2, at] = (grad_prod * key).astype(BF16)
                skip = skip + jnp.sum(
                    (grad_inner * product).reshape(LANES // 8, 8, LANES), axis=0
                )

        @pl.when(has_prev)
        def _():
            gm_copy(t).start()

        red_in[t] = jnp.concatenate(folds, axis=0)
        red_in[tiles + t // 8, pl.ds(lax.rem(t, 8), 1)] = jnp.sum(skip, axis=0, keepdims=True)
        sums = []
        for i in range(3):
            parts = [jnp.zeros((8, LANES), F32)] * 7
            for start in range(0, rows, CHUNK):
                grad = gm[t, i, pl.ds(start, CHUNK)].astype(F32)
                for j in range(7):
                    term = grad * padf[t, i, pl.ds(EDGE - j + start, CHUNK)]
                    parts[j] = parts[j] + jnp.sum(term.reshape(CHUNK // 8, 8, LANES), axis=0)
            sums += [jnp.sum(part, axis=0, keepdims=True) for part in parts]
            sums.append(jnp.zeros((1, LANES), F32))
        member = (
            lax.broadcasted_iota(jnp.int32, (LANES, LANES), 0) // 16 + t * 8
            == lax.broadcasted_iota(jnp.int32, (LANES, LANES), 1)
        ).astype(F32)
        return short_acc + jnp.dot(
            jnp.concatenate(sums, axis=0), member, precision=EXACT, preferred_element_type=F32
        )

    skip_units = (tiles + 7) // 8
    red_in[tiles:] = jnp.zeros((units - tiles, 8, LANES), F32)
    short_sum = lax.fori_loop(0, tiles, middle, jnp.zeros((24, LANES), F32))
    at_short = tiles + skip_units
    red_in[at_short : at_short + 3] = short_sum.reshape(3, 8, LANES)
    lags = red_in[:tiles].reshape(groups, LANES)
    lags = jnp.dot(lags, anti, precision=EXACT, preferred_element_type=F32)
    red_in[:tiles] = lags.reshape(tiles, 8, LANES)
    if reduce_here:
        for k in range(1, n):
            scatter_copy(k).start()
    else:
        red_out[...] = red_in[...]

    if reduce_here:
        total = red_in[pl.ds(me * share, share)]
        for k in range(1, n):
            scatter_copy(k).wait_recv()
            total = total + red_recv[k - 1]
        red_out[pl.ds(me * share, share)] = total
        for k in range(1, n):
            gather_copy(k).start()

    @pl.when(has_next)
    def _():
        edge_copy().wait_send()

    def drain(t, carry):
        @pl.when(has_next)
        def _():
            tail_copy(t).wait_send()
            gm_copy(t).wait_recv()

        @pl.when(has_prev)
        def _():
            head_copy(t).wait_send()
            gm_copy(t).wait_send()

        return carry

    lax.fori_loop(0, tiles, drain, 0)
    if reduce_here:
        for k in range(1, n):
            scatter_copy(k).wait_send()
            gather_copy(k).wait()


def finish(
    step_tiles,
    rows,
    group_scale,
    token_scale,
    gated_in,
    gm,
    red,
    taps_ref,
    gated_ref,
    fgrad_ref,
    long_ref,
    skip_ref,
    short_ref,
    gmf,
):
    groups = long_ref.shape[0]
    tiles = groups // 8
    skip_units = skip_ref.shape[0] // 8

    @pl.when(pl.program_id(0) == 0)
    def _():
        long_ref[...] = red[:tiles].reshape(groups, LANES) * group_scale
        skip_ref[...] = red[tiles : tiles + skip_units].reshape(skip_units * 8, LANES) * token_scale
        for i in range(3):
            short_ref[i] = red[tiles + skip_units + i][:7, :groups] * group_scale

    for u in range(step_tiles):
        cols = pl.ds(u * LANES, LANES)
        taps = tile_taps(taps_ref, pl.program_id(0) * step_tiles + u)
        gated_ref[:, cols] = gated_in[u]
        for i in range(3):
            gmf[i] = gm[u, i].astype(F32)
        for start in range(0, rows, CHUNK):
            for i in range(3):
                total = jnp.zeros((CHUNK, LANES), F32)
                for j in range(7):
                    total = total + taps[i][j : j + 1] * gmf[
                        i, pl.ds(start + j, CHUNK)
                    ]
                fgrad_ref[i, pl.ds(start, CHUNK), cols] = total.astype(BF16)


def body(features, short_taps, long_taps, skip_gain, cotangent):
    rows, width = features.shape[1:]
    tiles = width // LANES
    groups = width // 16
    n = lax.axis_size("ctx")
    skip_units = (tiles + 7) // 8
    units = tiles + skip_units + 3
    reduce_here = n <= 16
    if reduce_here:
        units = -(-units // n) * n
    share = units // n if reduce_here else 1
    peers = n - 1 if reduce_here else 1
    taps = jnp.transpose(short_taps, (0, 2, 1))
    vmem = pl.BlockSpec(memory_space=pltpu.VMEM)
    gated, grad_mixed, red = pl.pallas_call(
        functools.partial(kernel, n, tiles, rows, reduce_here),
        out_shape=(
            jax.ShapeDtypeStruct((tiles, rows, LANES), BF16),
            jax.ShapeDtypeStruct((tiles, 3, rows + EDGE, LANES), BF16),
            jax.ShapeDtypeStruct((units, 8, LANES), F32),
        ),
        in_specs=[vmem] * 5,
        out_specs=(vmem, vmem, vmem),
        scratch_shapes=[
            pltpu.VMEM((3, EDGE, width), BF16),
            pltpu.VMEM((tiles, 3, EDGE + rows, LANES), F32),
            pltpu.VMEM((tiles, 3, rows, LANES), BF16),
            pltpu.VMEM((tiles, LANES + rows, LANES), BF16),
            pltpu.VMEM((tiles, rows + LANES, LANES), BF16),
            pltpu.VMEM((tiles, 8, LANES, 2 * LANES), BF16),
            pltpu.VMEM((tiles, 8, LANES, 2 * LANES), BF16),
            pltpu.VMEM((groups, LANES), F32),
            pltpu.VMEM((tiles, LANES), F32),
            pltpu.VMEM((units, 8, LANES), F32),
            pltpu.VMEM((peers, share, 8, LANES), F32),
            pltpu.SemaphoreType.DMA((2, 1)),
            pltpu.SemaphoreType.DMA((2, tiles)),
            pltpu.SemaphoreType.DMA((2, tiles)),
            pltpu.SemaphoreType.DMA((2, tiles)),
            pltpu.SemaphoreType.DMA((2, peers)),
            pltpu.SemaphoreType.DMA((2, peers)),
        ],
        compiler_params=pltpu.CompilerParams(
            collective_id=0, has_side_effects=True, vmem_limit_bytes=60 * 1024 * 1024
        ),
        cost_estimate=pl.CostEstimate(
            flops=12 * rows * width * LANES * 8, bytes_accessed=16 * rows * width, transcendentals=0
        ),
    )(features, taps, long_taps, skip_gain.reshape(tiles, LANES), cotangent)
    if not reduce_here:
        red = lax.psum(red, "ctx")
    total = rows * n
    group_scale = 1.0 / math.sqrt(16.0 * total)
    token_scale = 1.0 / math.sqrt(1.0 * total)
    step_tiles = math.gcd(tiles, 4)
    span = step_tiles * LANES
    gated, fgrad, long_grad, skip_grad, short_grad = pl.pallas_call(
        functools.partial(finish, step_tiles, rows, group_scale, token_scale),
        grid=(tiles // step_tiles,),
        out_shape=(
            jax.ShapeDtypeStruct((rows, width), BF16),
            jax.ShapeDtypeStruct((3, rows, width), BF16),
            jax.ShapeDtypeStruct((groups, LANES), F32),
            jax.ShapeDtypeStruct((skip_units * 8, LANES), F32),
            jax.ShapeDtypeStruct((3, 7, groups), F32),
        ),
        in_specs=[
            pl.BlockSpec((step_tiles, rows, LANES), lambda t: (t, 0, 0)),
            pl.BlockSpec((step_tiles, 3, rows + EDGE, LANES), lambda t: (t, 0, 0, 0)),
            pl.BlockSpec((units, 8, LANES), lambda t: (0, 0, 0)),
            pl.BlockSpec((3, 7, groups), lambda t: (0, 0, 0)),
        ],
        out_specs=(
            pl.BlockSpec((rows, span), lambda t: (0, t)),
            pl.BlockSpec((3, rows, span), lambda t: (0, 0, t)),
            pl.BlockSpec((groups, LANES), lambda t: (0, 0)),
            pl.BlockSpec((skip_units * 8, LANES), lambda t: (0, 0)),
            pl.BlockSpec((3, 7, groups), lambda t: (0, 0, 0)),
        ),
        scratch_shapes=[pltpu.VMEM((3, rows + EDGE, LANES), F32)],
        compiler_params=pltpu.CompilerParams(vmem_limit_bytes=60 * 1024 * 1024),
    )(gated, grad_mixed, red, taps)
    short_grad = jnp.transpose(short_grad, (0, 2, 1))
    return gated, fgrad, short_grad, long_grad, skip_grad.reshape(-1)[:width]


def solution(mesh):
    placed = (P(None, "ctx", "tp"), P(None, "tp", None), P("tp", None), P("tp"), P("ctx", "tp"))
    return jax.shard_map(
        body,
        mesh=mesh,
        in_specs=placed,
        out_specs=(
            P("ctx", "tp"),
            P(None, "ctx", "tp"),
            P(None, "tp", None),
            P("tp", None),
            P("tp"),
        ),
        check_vma=False,
    )
```

```python
import functools
import math

import jax
import jax.numpy as jnp
from jax import lax
from jax.experimental import pallas as pl
from jax.experimental.pallas import tpu as pltpu
from jax.sharding import PartitionSpec as P

F32 = jnp.float32
BF16 = jnp.bfloat16
LANES = 128
EDGE = 16
CHUNK = 64
MESH = pl.DeviceIdType.MESH
EXACT = lax.Precision.HIGHEST


def lanes_of(tile):
    return pl.ds(pl.multiple_of(tile * LANES, LANES), LANES)


def tile_taps(taps_ref, tile, out):
    groups = taps_ref.shape[2]
    member = (
        lax.broadcasted_iota(jnp.int32, (groups, LANES), 0)
        == lax.broadcasted_iota(jnp.int32, (groups, LANES), 1) // 16 + tile * 8
    ).astype(F32).astype(BF16)
    for i in range(3):
        out[i, :7] = jnp.dot(taps_ref[i], member, preferred_element_type=F32)


def circulant(row, shift):
    return pltpu.roll(
        jnp.broadcast_to(row, (LANES, LANES)), shift, 1, stride=1, stride_axis=0
    )


def kernel(
    n,
    tiles,
    rows,
    reduce_here,
    feat_ref,
    taps_ref,
    long_ref,
    gain_ref,
    cot_ref,
    gated_ref,
    gm,
    red_out,
    edge,
    padf,
    mixed,
    prod,
    gi,
    causal,
    ahead,
    flipped,
    gainf,
    taps,
    red_in,
    red_recv,
    edge_sem,
    tail_sem,
    head_sem,
    gm_sem,
    scatter_sem,
    gather_sem,
):
    me = lax.axis_index("ctx")
    nxt = lax.rem(me + 1, n)
    prv = lax.rem(me + n - 1, n)
    has_prev = me > 0
    has_next = me < n - 1
    groups = 8 * tiles
    units = red_out.shape[0]
    share = units // n if reduce_here else 0

    def remote(src, dst, sems, index, device):
        return pltpu.make_async_remote_copy(
            src_ref=src,
            dst_ref=dst,
            send_sem=sems.at[0, index],
            recv_sem=sems.at[1, index],
            device_id={"ctx": device},
            device_id_type=MESH,
        )

    def edge_copy():
        return remote(feat_ref.at[:, pl.ds(rows - EDGE, EDGE)], edge, edge_sem, 0, nxt)

    def tail_copy(t):
        return remote(
            prod.at[t, pl.ds(rows, LANES)], prod.at[t, pl.ds(0, LANES)], tail_sem, t, nxt
        )

    def head_copy(t):
        return remote(gi.at[t, pl.ds(0, LANES)], gi.at[t, pl.ds(rows, LANES)], head_sem, t, prv)

    def gm_copy(t):
        return remote(
            gm.at[t, :, pl.ds(0, EDGE)], gm.at[t, :, pl.ds(rows, EDGE)], gm_sem, t, prv
        )

    def scatter_copy(k):
        peer = lax.rem(me + k, n)
        return remote(
            red_in.at[pl.ds(peer * share, share)], red_recv.at[k - 1], scatter_sem, k - 1, peer
        )

    def gather_copy(k):
        peer = lax.rem(me + k, n)
        mine = red_out.at[pl.ds(me * share, share)]
        return remote(mine, mine, gather_sem, k - 1, peer)

    barrier = pltpu.get_barrier_semaphore()
    if reduce_here:
        for k in range(1, n):
            pl.semaphore_signal(
                barrier, inc=1, device_id={"ctx": lax.rem(me + k, n)}, device_id_type=MESH
            )
        pl.semaphore_wait(barrier, n - 1)
    else:

        @pl.when(has_prev)
        def _():
            pl.semaphore_signal(barrier, inc=1, device_id={"ctx": prv}, device_id_type=MESH)

        @pl.when(has_next)
        def _():
            pl.semaphore_signal(barrier, inc=1, device_id={"ctx": nxt}, device_id_type=MESH)

        @pl.when(has_prev)
        def _():
            pl.semaphore_wait(barrier, 1)

        @pl.when(has_next)
        def _():
            pl.semaphore_wait(barrier, 1)

    @pl.when(has_next)
    def _():
        edge_copy().start()

    @pl.when(jnp.logical_not(has_prev))
    def _():
        edge[...] = jnp.zeros_like(edge)
        prod[:, :LANES] = jnp.zeros((tiles, LANES, LANES), BF16)

    @pl.when(jnp.logical_not(has_next))
    def _():
        gi[:, rows:] = jnp.zeros((tiles, LANES, LANES), BF16)
        gm[:, :, rows:] = jnp.zeros((tiles, 3, EDGE, LANES), BF16)

    row_pos = lax.broadcasted_iota(jnp.int32, (LANES, LANES), 0)
    col_pos = lax.broadcasted_iota(jnp.int32, (LANES, LANES), 1)
    above = col_pos > row_pos
    below = col_pos < row_pos
    past = col_pos + row_pos > LANES - 1
    anti = (row_pos + col_pos == LANES - 1).astype(F32)
    anti_b = anti.astype(BF16)
    flipped[...] = jnp.dot(long_ref[...], anti_b, preferred_element_type=F32)

    def build_causal(t, carry):
        part = flipped[pl.ds(pl.multiple_of(t * 8, 8), 8), :]
        for g in range(8):
            turned = circulant(part[g : g + 1], 1)
            causal[t, g, :, :LANES] = jnp.where(above, turned, 0.0).astype(BF16)
            causal[t, g, :, LANES:] = jnp.where(above, 0.0, turned).astype(BF16)
        return carry

    lax.fori_loop(0, tiles, build_causal, 0)

    @pl.when(has_prev)
    def _():
        edge_copy().wait_recv()

    gainf[...] = gain_ref[...].astype(F32)

    def front(t, carry):
        cols = lanes_of(t)
        tile_taps(taps_ref, t, taps)
        for i in range(3):
            padf[t, i, :EDGE] = edge[i, :, cols].astype(F32)
            padf[t, i, EDGE:] = feat_ref[i, :, cols].astype(F32)
        for start in range(0, rows, CHUNK):
            values = []
            for i in range(3):
                total = jnp.zeros((CHUNK, LANES), F32)
                for j in range(7):
                    total = total + taps[i, pl.ds(j, 1)] * padf[
                        t, i, pl.ds(EDGE - j + start, CHUNK)
                    ]
                rounded = total.astype(BF16)
                mixed[t, i, pl.ds(start, CHUNK)] = rounded
                values.append(rounded.astype(F32))
            query, key, value = values
            prod[t, pl.ds(LANES + start, CHUNK)] = (key * value).astype(BF16)
            grad_in = cot_ref[pl.ds(start, CHUNK), cols].astype(F32)
            gi[t, pl.ds(start, CHUNK)] = (grad_in * query).astype(BF16)

        @pl.when(has_next)
        def _():
            tail_copy(t).start()

        @pl.when(has_prev)
        def _():
            head_copy(t).start()

        return carry

    lax.fori_loop(0, tiles, front, 0)

    flipped[...] = long_ref[...].astype(F32)

    def build_ahead(t, carry):
        part = flipped[pl.ds(pl.multiple_of(t * 8, 8), 8), :]
        for g in range(8):
            turned = circulant(part[g : g + 1], 0)
            ahead[t, g, :, :LANES] = jnp.where(below, 0.0, turned).astype(BF16)
            ahead[t, g, :, LANES:] = jnp.where(below, turned, 0.0).astype(BF16)
        return carry

    lax.fori_loop(0, tiles, build_ahead, 0)

    lane_group = lax.rem(
        lax.broadcasted_iota(jnp.int32, (LANES, 2 * LANES), 1), LANES
    ) // 16
    blocks = rows // LANES

    def pair(ref, t, first):
        return jnp.concatenate(
            [ref[t, pl.ds(first, LANES)], ref[t, pl.ds(first + LANES, LANES)]], axis=1
        )

    def middle(t, short_acc):
        cols = lanes_of(t)

        @pl.when(has_prev)
        def _():
            tail_copy(t).wait_recv()

        @pl.when(has_next)
        def _():
            head_copy(t).wait_recv()

        gain = gainf[pl.ds(t, 1)]
        skip = jnp.zeros((8, LANES), F32)
        folds = [jnp.zeros((1, LANES), F32)] * 8
        for first in range(0, rows, 2 * LANES):
            span = 2 * LANES
            window = jnp.concatenate(
                [prod[t, pl.ds(first, span)], prod[t, pl.ds(first + LANES, span)]], axis=1
            )
            coming = jnp.concatenate(
                [gi[t, pl.ds(first, span)], gi[t, pl.ds(first + LANES, span)]], axis=1
            )
            conv = jnp.zeros((LANES, 2 * LANES), F32)
            back = jnp.zeros((LANES, 2 * LANES), F32)
            turned = jnp.dot(anti_b, pair(gi, t, first), preferred_element_type=F32)
            ones = jnp.dot(
                causal[t].reshape(8 * LANES, span), window, preferred_element_type=F32
            )
            for g in range(8):
                conv = jnp.where(lane_group == g, ones[g * LANES : (g + 1) * LANES], conv)
            twos = jnp.dot(
                ahead[t].reshape(8 * LANES, span), coming, preferred_element_type=F32
            )
            for g in range(8):
                back = jnp.where(lane_group == g, twos[g * LANES : (g + 1) * LANES], back)
            apart = [jnp.where(lane_group == g, turned, 0.0).astype(BF16) for g in range(8)]
            grids = lax.dot_general(
                jnp.concatenate(apart, axis=0),
                window,
                (((1,), (1,)), ((), ())),
                preferred_element_type=F32,
            )
            for g in range(8):
                grid = grids[g * LANES : (g + 1) * LANES]
                ring = jnp.where(past, grid[:, :LANES], grid[:, LANES:])
                lined = pltpu.roll(ring, 0, 1, stride=1, stride_axis=0)
                folds[g] = folds[g] + jnp.sum(lined, axis=0, keepdims=True)
            for half in range(2):
                start = first + half * LANES
                here = slice(half * LANES, (half + 1) * LANES)
                at = pl.ds(start, LANES)
                product = prod[t, pl.ds(start + LANES, LANES)].astype(F32)
                grad_inner = gi[t, at].astype(F32)
                query = mixed[t, 0, at].astype(F32)
                key = mixed[t, 1, at].astype(F32)
                value = mixed[t, 2, at].astype(F32)
                inner = conv[:, here] + gain * product
                gated_ref[t, at] = (query * inner).astype(BF16)
                gm[t, 0, at] = (cot_ref[at, cols].astype(F32) * inner).astype(BF16)
                grad_prod = (back[:, here] + gain * grad_inner).astype(BF16).astype(F32)
                gm[t, 1, at] = (grad_prod * value).astype(BF16)
                gm[t, 2, at] = (grad_prod * key).astype(BF16)
                skip = skip + jnp.sum(
                    (grad_inner * product).reshape(LANES // 8, 8, LANES), axis=0
                )

        @pl.when(has_prev)
        def _():
            gm_copy(t).start()

        red_in[t] = jnp.concatenate(folds, axis=0)
        red_in[tiles + t // 8, pl.ds(lax.rem(t, 8), 1)] = jnp.sum(skip, axis=0, keepdims=True)
        sums = []
        for i in range(3):
            parts = [jnp.zeros((8, LANES), F32)] * 7
            for start in range(0, rows, CHUNK):
                grad = gm[t, i, pl.ds(start, CHUNK)].astype(F32)
                for j in range(7):
                    term = grad * padf[t, i, pl.ds(EDGE - j + start, CHUNK)]
                    parts[j] = parts[j] + jnp.sum(term.reshape(CHUNK // 8, 8, LANES), axis=0)
            sums += [jnp.sum(part, axis=0, keepdims=True) for part in parts]
            sums.append(jnp.zeros((1, LANES), F32))
        member = (
            lax.broadcasted_iota(jnp.int32, (LANES, LANES), 0) // 16 + t * 8
            == lax.broadcasted_iota(jnp.int32, (LANES, LANES), 1)
        ).astype(F32)
        return short_acc + jnp.dot(
            jnp.concatenate(sums, axis=0), member, precision=EXACT, preferred_element_type=F32
        )

    skip_units = (tiles + 7) // 8
    red_in[tiles:] = jnp.zeros((units - tiles, 8, LANES), F32)
    short_sum = lax.fori_loop(0, tiles, middle, jnp.zeros((24, LANES), F32))
    at_short = tiles + skip_units
    red_in[at_short : at_short + 3] = short_sum.reshape(3, 8, LANES)
    lags = red_in[:tiles].reshape(groups, LANES)
    lags = jnp.dot(lags, anti, precision=EXACT, preferred_element_type=F32)
    red_in[:tiles] = lags.reshape(tiles, 8, LANES)
    if reduce_here:
        for k in range(1, n):
            scatter_copy(k).start()
    else:
        red_out[...] = red_in[...]

    if reduce_here:
        total = red_in[pl.ds(me * share, share)]
        for k in range(1, n):
            scatter_copy(k).wait_recv()
            total = total + red_recv[k - 1]
        red_out[pl.ds(me * share, share)] = total
        for k in range(1, n):
            gather_copy(k).start()

    @pl.when(has_next)
    def _():
        edge_copy().wait_send()

    def drain(t, carry):
        @pl.when(has_next)
        def _():
            tail_copy(t).wait_send()
            gm_copy(t).wait_recv()

        @pl.when(has_prev)
        def _():
            head_copy(t).wait_send()
            gm_copy(t).wait_send()

        return carry

    lax.fori_loop(0, tiles, drain, 0)
    if reduce_here:
        for k in range(1, n):
            scatter_copy(k).wait_send()
            gather_copy(k).wait()


def finish(
    step_tiles,
    rows,
    group_scale,
    token_scale,
    gated_in,
    gm,
    red,
    taps_ref,
    gated_ref,
    fgrad_ref,
    long_ref,
    skip_ref,
    short_ref,
    gmf,
    taps,
):
    groups = long_ref.shape[0]
    tiles = groups // 8
    skip_units = skip_ref.shape[0] // 8

    @pl.when(pl.program_id(0) == 0)
    def _():
        long_ref[...] = red[:tiles].reshape(groups, LANES) * group_scale
        skip_ref[...] = red[tiles : tiles + skip_units].reshape(skip_units * 8, LANES) * token_scale
        for i in range(3):
            short_ref[i] = red[tiles + skip_units + i][:7, :groups] * group_scale

    for u in range(step_tiles):
        cols = pl.ds(u * LANES, LANES)
        tile_taps(taps_ref, pl.program_id(0) * step_tiles + u, taps)
        gated_ref[:, cols] = gated_in[u]
        for i in range(3):
            gmf[i] = gm[u, i].astype(F32)
        for start in range(0, rows, CHUNK):
            for i in range(3):
                total = jnp.zeros((CHUNK, LANES), F32)
                for j in range(7):
                    total = total + taps[i, pl.ds(j, 1)] * gmf[
                        i, pl.ds(start + j, CHUNK)
                    ]
                fgrad_ref[i, pl.ds(start, CHUNK), cols] = total.astype(BF16)


def body(features, short_taps, long_taps, skip_gain, cotangent):
    rows, width = features.shape[1:]
    tiles = width // LANES
    groups = width // 16
    n = lax.axis_size("ctx")
    skip_units = (tiles + 7) // 8
    units = tiles + skip_units + 3
    reduce_here = n <= 16
    if reduce_here:
        units = -(-units // n) * n
    share = units // n if reduce_here else 1
    peers = n - 1 if reduce_here else 1
    taps = jnp.transpose(short_taps, (0, 2, 1))
    vmem = pl.BlockSpec(memory_space=pltpu.VMEM)
    gated, grad_mixed, red = pl.pallas_call(
        functools.partial(kernel, n, tiles, rows, reduce_here),
        out_shape=(
            jax.ShapeDtypeStruct((tiles, rows, LANES), BF16),
            jax.ShapeDtypeStruct((tiles, 3, rows + EDGE, LANES), BF16),
            jax.ShapeDtypeStruct((units, 8, LANES), F32),
        ),
        in_specs=[vmem] * 5,
        out_specs=(vmem, vmem, vmem),
        scratch_shapes=[
            pltpu.VMEM((3, EDGE, width), BF16),
            pltpu.VMEM((tiles, 3, EDGE + rows, LANES), F32),
            pltpu.VMEM((tiles, 3, rows, LANES), BF16),
            pltpu.VMEM((tiles, LANES + rows, LANES), BF16),
            pltpu.VMEM((tiles, rows + LANES, LANES), BF16),
            pltpu.VMEM((tiles, 8, LANES, 2 * LANES), BF16),
            pltpu.VMEM((tiles, 8, LANES, 2 * LANES), BF16),
            pltpu.VMEM((groups, LANES), F32),
            pltpu.VMEM((tiles, LANES), F32),
            pltpu.VMEM((3, 8, LANES), F32),
            pltpu.VMEM((units, 8, LANES), F32),
            pltpu.VMEM((peers, share, 8, LANES), F32),
            pltpu.SemaphoreType.DMA((2, 1)),
            pltpu.SemaphoreType.DMA((2, tiles)),
            pltpu.SemaphoreType.DMA((2, tiles)),
            pltpu.SemaphoreType.DMA((2, tiles)),
            pltpu.SemaphoreType.DMA((2, peers)),
            pltpu.SemaphoreType.DMA((2, peers)),
        ],
        compiler_params=pltpu.CompilerParams(
            collective_id=0, has_side_effects=True, vmem_limit_bytes=60 * 1024 * 1024
        ),
        cost_estimate=pl.CostEstimate(
            flops=12 * rows * width * LANES * 8, bytes_accessed=16 * rows * width, transcendentals=0
        ),
    )(features, taps, long_taps, skip_gain.reshape(tiles, LANES), cotangent)
    if not reduce_here:
        red = lax.psum(red, "ctx")
    total = rows * n
    group_scale = 1.0 / math.sqrt(16.0 * total)
    token_scale = 1.0 / math.sqrt(1.0 * total)
    step_tiles = math.gcd(tiles, 4)
    span = step_tiles * LANES
    gated, fgrad, long_grad, skip_grad, short_grad = pl.pallas_call(
        functools.partial(finish, step_tiles, rows, group_scale, token_scale),
        grid=(tiles // step_tiles,),
        out_shape=(
            jax.ShapeDtypeStruct((rows, width), BF16),
            jax.ShapeDtypeStruct((3, rows, width), BF16),
            jax.ShapeDtypeStruct((groups, LANES), F32),
            jax.ShapeDtypeStruct((skip_units * 8, LANES), F32),
            jax.ShapeDtypeStruct((3, 7, groups), F32),
        ),
        in_specs=[
            pl.BlockSpec((step_tiles, rows, LANES), lambda t: (t, 0, 0)),
            pl.BlockSpec((step_tiles, 3, rows + EDGE, LANES), lambda t: (t, 0, 0, 0)),
            pl.BlockSpec((units, 8, LANES), lambda t: (0, 0, 0)),
            pl.BlockSpec((3, 7, groups), lambda t: (0, 0, 0)),
        ],
        out_specs=(
            pl.BlockSpec((rows, span), lambda t: (0, t)),
            pl.BlockSpec((3, rows, span), lambda t: (0, 0, t)),
            pl.BlockSpec((groups, LANES), lambda t: (0, 0)),
            pl.BlockSpec((skip_units * 8, LANES), lambda t: (0, 0)),
            pl.BlockSpec((3, 7, groups), lambda t: (0, 0, 0)),
        ),
        scratch_shapes=[
            pltpu.VMEM((3, rows + EDGE, LANES), F32),
            pltpu.VMEM((3, 8, LANES), F32),
        ],
        compiler_params=pltpu.CompilerParams(vmem_limit_bytes=60 * 1024 * 1024),
    )(gated, grad_mixed, red, taps)
    short_grad = jnp.transpose(short_grad, (0, 2, 1))
    return gated, fgrad, short_grad, long_grad, skip_grad.reshape(-1)[:width]


def solution(mesh):
    placed = (P(None, "ctx", "tp"), P(None, "tp", None), P("tp", None), P("tp"), P("ctx", "tp"))
    return jax.shard_map(
        body,
        mesh=mesh,
        in_specs=placed,
        out_specs=(
            P("ctx", "tp"),
            P(None, "ctx", "tp"),
            P(None, "tp", None),
            P("tp", None),
            P("tp"),
        ),
        check_vma=False,
    )
```

```python
import functools
import math

import jax
import jax.numpy as jnp
from jax import lax
from jax.experimental import pallas as pl
from jax.experimental.pallas import tpu as pltpu
from jax.sharding import PartitionSpec as P

F32 = jnp.float32
BF16 = jnp.bfloat16
LANES = 128
EDGE = 16
CHUNK = 64
MESH = pl.DeviceIdType.MESH
EXACT = lax.Precision.HIGHEST


def lanes_of(tile):
    return pl.ds(pl.multiple_of(tile * LANES, LANES), LANES)


def tile_taps(taps_ref, tile, out):
    groups = taps_ref.shape[2]
    member = (
        lax.broadcasted_iota(jnp.int32, (groups, LANES), 0)
        == lax.broadcasted_iota(jnp.int32, (groups, LANES), 1) // 16 + tile * 8
    ).astype(F32).astype(BF16)
    found = [jnp.dot(taps_ref[i], member, preferred_element_type=F32) for i in range(3)]
    if out is not None:
        for i in range(3):
            out[i, :7] = found[i]
    return found


def circulant(row, shift):
    return pltpu.roll(
        jnp.broadcast_to(row, (LANES, LANES)), shift, 1, stride=1, stride_axis=0
    )


def kernel(
    n,
    tiles,
    rows,
    reduce_here,
    feat_ref,
    taps_ref,
    long_ref,
    gain_ref,
    cot_ref,
    gated_ref,
    gm,
    red_out,
    edge,
    padf,
    mixed,
    prod,
    gi,
    causal,
    ahead,
    flipped,
    gainf,
    taps,
    red_in,
    red_recv,
    edge_sem,
    tail_sem,
    head_sem,
    gm_sem,
    scatter_sem,
    gather_sem,
):
    me = lax.axis_index("ctx")
    nxt = lax.rem(me + 1, n)
    prv = lax.rem(me + n - 1, n)
    has_prev = me > 0
    has_next = me < n - 1
    groups = 8 * tiles
    units = red_out.shape[0]
    share = units // n if reduce_here else 0

    def remote(src, dst, sems, index, device):
        return pltpu.make_async_remote_copy(
            src_ref=src,
            dst_ref=dst,
            send_sem=sems.at[0, index],
            recv_sem=sems.at[1, index],
            device_id={"ctx": device},
            device_id_type=MESH,
        )

    def edge_copy():
        return remote(feat_ref.at[:, pl.ds(rows - EDGE, EDGE)], edge, edge_sem, 0, nxt)

    def tail_copy(t):
        return remote(
            prod.at[t, pl.ds(rows, LANES)], prod.at[t, pl.ds(0, LANES)], tail_sem, t, nxt
        )

    def head_copy(t):
        return remote(gi.at[t, pl.ds(0, LANES)], gi.at[t, pl.ds(rows, LANES)], head_sem, t, prv)

    def gm_copy(t):
        return remote(
            gm.at[t, :, pl.ds(0, EDGE)], gm.at[t, :, pl.ds(rows, EDGE)], gm_sem, t, prv
        )

    def scatter_copy(k):
        peer = lax.rem(me + k, n)
        return remote(
            red_in.at[pl.ds(peer * share, share)], red_recv.at[k - 1], scatter_sem, k - 1, peer
        )

    def gather_copy(k):
        peer = lax.rem(me + k, n)
        mine = red_out.at[pl.ds(me * share, share)]
        return remote(mine, mine, gather_sem, k - 1, peer)

    barrier = pltpu.get_barrier_semaphore()
    if reduce_here:
        for k in range(1, n):
            pl.semaphore_signal(
                barrier, inc=1, device_id={"ctx": lax.rem(me + k, n)}, device_id_type=MESH
            )
        pl.semaphore_wait(barrier, n - 1)
    else:

        @pl.when(has_prev)
        def _():
            pl.semaphore_signal(barrier, inc=1, device_id={"ctx": prv}, device_id_type=MESH)

        @pl.when(has_next)
        def _():
            pl.semaphore_signal(barrier, inc=1, device_id={"ctx": nxt}, device_id_type=MESH)

        @pl.when(has_prev)
        def _():
            pl.semaphore_wait(barrier, 1)

        @pl.when(has_next)
        def _():
            pl.semaphore_wait(barrier, 1)

    @pl.when(has_next)
    def _():
        edge_copy().start()

    @pl.when(jnp.logical_not(has_prev))
    def _():
        edge[...] = jnp.zeros_like(edge)
        prod[:, :LANES] = jnp.zeros((tiles, LANES, LANES), BF16)

    @pl.when(jnp.logical_not(has_next))
    def _():
        gi[:, rows:] = jnp.zeros((tiles, LANES, LANES), BF16)
        gm[:, :, rows:] = jnp.zeros((tiles, 3, EDGE, LANES), BF16)

    row_pos = lax.broadcasted_iota(jnp.int32, (LANES, LANES), 0)
    col_pos = lax.broadcasted_iota(jnp.int32, (LANES, LANES), 1)
    above = col_pos > row_pos
    below = col_pos < row_pos
    past = col_pos + row_pos > LANES - 1
    anti = (row_pos + col_pos == LANES - 1).astype(F32)
    anti_b = anti.astype(BF16)
    flipped[...] = jnp.dot(long_ref[...], anti_b, preferred_element_type=F32)

    def build_causal(t, carry):
        part = flipped[pl.ds(pl.multiple_of(t * 8, 8), 8), :]
        for g in range(8):
            turned = circulant(part[g : g + 1], 1)
            causal[t, g, :, :LANES] = jnp.where(above, turned, 0.0).astype(BF16)
            causal[t, g, :, LANES:] = jnp.where(above, 0.0, turned).astype(BF16)
        return carry

    lax.fori_loop(0, tiles, build_causal, 0)

    @pl.when(has_prev)
    def _():
        edge_copy().wait_recv()

    gainf[...] = gain_ref[...].astype(F32)

    def front(t, carry):
        cols = lanes_of(t)
        tile_taps(taps_ref, t, taps)
        for i in range(3):
            padf[t, i, :EDGE] = edge[i, :, cols].astype(F32)
            padf[t, i, EDGE:] = feat_ref[i, :, cols].astype(F32)
        for start in range(0, rows, CHUNK):
            values = []
            for i in range(3):
                total = jnp.zeros((CHUNK, LANES), F32)
                for j in range(7):
                    total = total + taps[i, pl.ds(j, 1)] * padf[
                        t, i, pl.ds(EDGE - j + start, CHUNK)
                    ]
                rounded = total.astype(BF16)
                mixed[t, i, pl.ds(start, CHUNK)] = rounded
                values.append(rounded.astype(F32))
            query, key, value = values
            prod[t, pl.ds(LANES + start, CHUNK)] = (key * value).astype(BF16)
            grad_in = cot_ref[pl.ds(start, CHUNK), cols].astype(F32)
            gi[t, pl.ds(start, CHUNK)] = (grad_in * query).astype(BF16)

        @pl.when(has_next)
        def _():
            tail_copy(t).start()

        @pl.when(has_prev)
        def _():
            head_copy(t).start()

        return carry

    lax.fori_loop(0, tiles, front, 0)

    flipped[...] = long_ref[...].astype(F32)

    def build_ahead(t, carry):
        part = flipped[pl.ds(pl.multiple_of(t * 8, 8), 8), :]
        for g in range(8):
            turned = circulant(part[g : g + 1], 0)
            ahead[t, g, :, :LANES] = jnp.where(below, 0.0, turned).astype(BF16)
            ahead[t, g, :, LANES:] = jnp.where(below, turned, 0.0).astype(BF16)
        return carry

    lax.fori_loop(0, tiles, build_ahead, 0)

    lane_group = lax.rem(
        lax.broadcasted_iota(jnp.int32, (LANES, 2 * LANES), 1), LANES
    ) // 16
    blocks = rows // LANES

    def pair(ref, t, first):
        return jnp.concatenate(
            [ref[t, pl.ds(first, LANES)], ref[t, pl.ds(first + LANES, LANES)]], axis=1
        )

    def middle(t, short_acc):
        cols = lanes_of(t)

        @pl.when(has_prev)
        def _():
            tail_copy(t).wait_recv()

        @pl.when(has_next)
        def _():
            head_copy(t).wait_recv()

        gain = gainf[pl.ds(t, 1)]
        skip = jnp.zeros((8, LANES), F32)
        folds = [jnp.zeros((1, LANES), F32)] * 8
        for first in range(0, rows, 2 * LANES):
            span = 2 * LANES
            window = jnp.concatenate(
                [prod[t, pl.ds(first, span)], prod[t, pl.ds(first + LANES, span)]], axis=1
            )
            coming = jnp.concatenate(
                [gi[t, pl.ds(first, span)], gi[t, pl.ds(first + LANES, span)]], axis=1
            )
            conv = jnp.zeros((LANES, 2 * LANES), F32)
            back = jnp.zeros((LANES, 2 * LANES), F32)
            turned = jnp.dot(anti_b, pair(gi, t, first), preferred_element_type=F32)
            ones = jnp.dot(
                causal[t].reshape(8 * LANES, span), window, preferred_element_type=F32
            )
            for g in range(8):
                conv = jnp.where(lane_group == g, ones[g * LANES : (g + 1) * LANES], conv)
            twos = jnp.dot(
                ahead[t].reshape(8 * LANES, span), coming, preferred_element_type=F32
            )
            for g in range(8):
                back = jnp.where(lane_group == g, twos[g * LANES : (g + 1) * LANES], back)
            apart = [jnp.where(lane_group == g, turned, 0.0).astype(BF16) for g in range(8)]
            grids = lax.dot_general(
                jnp.concatenate(apart, axis=0),
                window,
                (((1,), (1,)), ((), ())),
                preferred_element_type=F32,
            )
            for g in range(8):
                grid = grids[g * LANES : (g + 1) * LANES]
                ring = jnp.where(past, grid[:, :LANES], grid[:, LANES:])
                lined = pltpu.roll(ring, 0, 1, stride=1, stride_axis=0)
                folds[g] = folds[g] + jnp.sum(lined, axis=0, keepdims=True)
            for half in range(2):
                start = first + half * LANES
                here = slice(half * LANES, (half + 1) * LANES)
                at = pl.ds(start, LANES)
                product = prod[t, pl.ds(start + LANES, LANES)].astype(F32)
                grad_inner = gi[t, at].astype(F32)
                query = mixed[t, 0, at].astype(F32)
                key = mixed[t, 1, at].astype(F32)
                value = mixed[t, 2, at].astype(F32)
                inner = conv[:, here] + gain * product
                gated_ref[t, at] = (query * inner).astype(BF16)
                gm[t, 0, at] = (cot_ref[at, cols].astype(F32) * inner).astype(BF16)
                grad_prod = (back[:, here] + gain * grad_inner).astype(BF16).astype(F32)
                gm[t, 1, at] = (grad_prod * value).astype(BF16)
                gm[t, 2, at] = (grad_prod * key).astype(BF16)
                skip = skip + jnp.sum(
                    (grad_inner * product).reshape(LANES // 8, 8, LANES), axis=0
                )

        red_in[t] = jnp.concatenate(folds, axis=0)
        red_in[tiles + t // 8, pl.ds(lax.rem(t, 8), 1)] = jnp.sum(skip, axis=0, keepdims=True)
        sums = []
        for i in range(3):
            parts = [jnp.zeros((8, LANES), F32)] * 7
            for start in range(0, rows, CHUNK):
                grad = gm[t, i, pl.ds(start, CHUNK)].astype(F32)
                for j in range(7):
                    term = grad * padf[t, i, pl.ds(EDGE - j + start, CHUNK)]
                    parts[j] = parts[j] + jnp.sum(term.reshape(CHUNK // 8, 8, LANES), axis=0)
            sums += [jnp.sum(part, axis=0, keepdims=True) for part in parts]
            sums.append(jnp.zeros((1, LANES), F32))
        member = (
            lax.broadcasted_iota(jnp.int32, (LANES, LANES), 0) // 16 + t * 8
            == lax.broadcasted_iota(jnp.int32, (LANES, LANES), 1)
        ).astype(F32)
        short_acc = short_acc + jnp.dot(
            jnp.concatenate(sums, axis=0), member, precision=EXACT, preferred_element_type=F32
        )

        @pl.when(has_prev)
        def _():
            gm_copy(t).start()

        return short_acc

    skip_units = (tiles + 7) // 8
    red_in[tiles:] = jnp.zeros((units - tiles, 8, LANES), F32)
    short_sum = lax.fori_loop(0, tiles, middle, jnp.zeros((24, LANES), F32))
    at_short = tiles + skip_units
    red_in[at_short : at_short + 3] = short_sum.reshape(3, 8, LANES)
    lags = red_in[:tiles].reshape(groups, LANES)
    lags = jnp.dot(lags, anti, precision=EXACT, preferred_element_type=F32)
    red_in[:tiles] = lags.reshape(tiles, 8, LANES)
    if reduce_here:
        for k in range(1, n):
            scatter_copy(k).start()
    else:
        red_out[...] = red_in[...]

    if reduce_here:
        total = red_in[pl.ds(me * share, share)]
        for k in range(1, n):
            scatter_copy(k).wait_recv()
            total = total + red_recv[k - 1]
        red_out[pl.ds(me * share, share)] = total
        for k in range(1, n):
            gather_copy(k).start()

    @pl.when(has_next)
    def _():
        edge_copy().wait_send()

    def drain(t, carry):
        @pl.when(has_next)
        def _():
            tail_copy(t).wait_send()
            gm_copy(t).wait_recv()

        @pl.when(has_prev)
        def _():
            head_copy(t).wait_send()
            gm_copy(t).wait_send()

        return carry

    lax.fori_loop(0, tiles, drain, 0)
    if reduce_here:
        for k in range(1, n):
            scatter_copy(k).wait_send()
            gather_copy(k).wait()


def finish(
    step_tiles,
    rows,
    group_scale,
    token_scale,
    gated_in,
    gm,
    red,
    taps_ref,
    gated_ref,
    fgrad_ref,
    long_ref,
    skip_ref,
    short_ref,
    gmf,
):
    groups = long_ref.shape[0]
    tiles = groups // 8
    skip_units = skip_ref.shape[0] // 8

    @pl.when(pl.program_id(0) == 0)
    def _():
        long_ref[...] = red[:tiles].reshape(groups, LANES) * group_scale
        skip_ref[...] = red[tiles : tiles + skip_units].reshape(skip_units * 8, LANES) * token_scale
        for i in range(3):
            short_ref[i] = red[tiles + skip_units + i][:7, :groups] * group_scale

    for u in range(step_tiles):
        cols = pl.ds(u * LANES, LANES)
        taps = tile_taps(taps_ref, pl.program_id(0) * step_tiles + u, None)
        gated_ref[:, cols] = gated_in[u]
        for i in range(3):
            gmf[i] = gm[u, i].astype(F32)
        for start in range(0, rows, CHUNK):
            for i in range(3):
                total = jnp.zeros((CHUNK, LANES), F32)
                for j in range(7):
                    total = total + taps[i][j : j + 1] * gmf[
                        i, pl.ds(start + j, CHUNK)
                    ]
                fgrad_ref[i, pl.ds(start, CHUNK), cols] = total.astype(BF16)


def body(features, short_taps, long_taps, skip_gain, cotangent):
    rows, width = features.shape[1:]
    tiles = width // LANES
    groups = width // 16
    n = lax.axis_size("ctx")
    skip_units = (tiles + 7) // 8
    units = tiles + skip_units + 3
    reduce_here = n <= 16
    if reduce_here:
        units = -(-units // n) * n
    share = units // n if reduce_here else 1
    peers = n - 1 if reduce_here else 1
    taps = jnp.transpose(short_taps, (0, 2, 1))
    vmem = pl.BlockSpec(memory_space=pltpu.VMEM)
    gated, grad_mixed, red = pl.pallas_call(
        functools.partial(kernel, n, tiles, rows, reduce_here),
        out_shape=(
            jax.ShapeDtypeStruct((tiles, rows, LANES), BF16),
            jax.ShapeDtypeStruct((tiles, 3, rows + EDGE, LANES), BF16),
            jax.ShapeDtypeStruct((units, 8, LANES), F32),
        ),
        in_specs=[vmem] * 5,
        out_specs=(vmem, vmem, vmem),
        scratch_shapes=[
            pltpu.VMEM((3, EDGE, width), BF16),
            pltpu.VMEM((tiles, 3, EDGE + rows, LANES), F32),
            pltpu.VMEM((tiles, 3, rows, LANES), BF16),
            pltpu.VMEM((tiles, LANES + rows, LANES), BF16),
            pltpu.VMEM((tiles, rows + LANES, LANES), BF16),
            pltpu.VMEM((tiles, 8, LANES, 2 * LANES), BF16),
            pltpu.VMEM((tiles, 8, LANES, 2 * LANES), BF16),
            pltpu.VMEM((groups, LANES), F32),
            pltpu.VMEM((tiles, LANES), F32),
            pltpu.VMEM((3, 8, LANES), F32),
            pltpu.VMEM((units, 8, LANES), F32),
            pltpu.VMEM((peers, share, 8, LANES), F32),
            pltpu.SemaphoreType.DMA((2, 1)),
            pltpu.SemaphoreType.DMA((2, tiles)),
            pltpu.SemaphoreType.DMA((2, tiles)),
            pltpu.SemaphoreType.DMA((2, tiles)),
            pltpu.SemaphoreType.DMA((2, peers)),
            pltpu.SemaphoreType.DMA((2, peers)),
        ],
        compiler_params=pltpu.CompilerParams(
            collective_id=0, has_side_effects=True, vmem_limit_bytes=60 * 1024 * 1024
        ),
        cost_estimate=pl.CostEstimate(
            flops=12 * rows * width * LANES * 8, bytes_accessed=16 * rows * width, transcendentals=0
        ),
    )(features, taps, long_taps, skip_gain.reshape(tiles, LANES), cotangent)
    if not reduce_here:
        red = lax.psum(red, "ctx")
    total = rows * n
    group_scale = 1.0 / math.sqrt(16.0 * total)
    token_scale = 1.0 / math.sqrt(1.0 * total)
    step_tiles = math.gcd(tiles, 4)
    span = step_tiles * LANES
    gated, fgrad, long_grad, skip_grad, short_grad = pl.pallas_call(
        functools.partial(finish, step_tiles, rows, group_scale, token_scale),
        grid=(tiles // step_tiles,),
        out_shape=(
            jax.ShapeDtypeStruct((rows, width), BF16),
            jax.ShapeDtypeStruct((3, rows, width), BF16),
            jax.ShapeDtypeStruct((groups, LANES), F32),
            jax.ShapeDtypeStruct((skip_units * 8, LANES), F32),
            jax.ShapeDtypeStruct((3, 7, groups), F32),
        ),
        in_specs=[
            pl.BlockSpec((step_tiles, rows, LANES), lambda t: (t, 0, 0)),
            pl.BlockSpec((step_tiles, 3, rows + EDGE, LANES), lambda t: (t, 0, 0, 0)),
            pl.BlockSpec((units, 8, LANES), lambda t: (0, 0, 0)),
            pl.BlockSpec((3, 7, groups), lambda t: (0, 0, 0)),
        ],
        out_specs=(
            pl.BlockSpec((rows, span), lambda t: (0, t)),
            pl.BlockSpec((3, rows, span), lambda t: (0, 0, t)),
            pl.BlockSpec((groups, LANES), lambda t: (0, 0)),
            pl.BlockSpec((skip_units * 8, LANES), lambda t: (0, 0)),
            pl.BlockSpec((3, 7, groups), lambda t: (0, 0, 0)),
        ),
        scratch_shapes=[
            pltpu.VMEM((3, rows + EDGE, LANES), F32),
        ],
        compiler_params=pltpu.CompilerParams(vmem_limit_bytes=60 * 1024 * 1024),
    )(gated, grad_mixed, red, taps)
    short_grad = jnp.transpose(short_grad, (0, 2, 1))
    return gated, fgrad, short_grad, long_grad, skip_grad.reshape(-1)[:width]


def solution(mesh):
    placed = (P(None, "ctx", "tp"), P(None, "tp", None), P("tp", None), P("tp"), P("ctx", "tp"))
    return jax.shard_map(
        body,
        mesh=mesh,
        in_specs=placed,
        out_specs=(
            P("ctx", "tp"),
            P(None, "ctx", "tp"),
            P(None, "tp", None),
            P("tp", None),
            P("tp"),
        ),
        check_vma=False,
    )
```
